32 devices in a mesh: head: 4 (over y, x), tok: 8 (over z, core).
Axes of the slice: x: 2, y: 2, z: 4, core: 2. Of those that a mesh axis runs over, the one named last changes fastest.
Arguments:
- tokens: bfloat16 [2048, 2048], P(('tok', 'head')), may hold values from -6 to 6
- token_req: int32 [2048], P(('tok', 'head')), may hold values from 0 to 1, as said below
- cache_len: int32 [16], P('tok'), may hold values from 16 to 1023, as said below
- sink_count: int32 [16], P('tok'), may hold values from 1 to 8
- cache_k: bfloat16 [16, 1024, 2048], P('tok', None, 'head'), may hold values from -64 to 64
- cache_v: bfloat16 [16, 1024, 2048], P('tok', None, 'head'), may hold values from -6 to 6
- attn_gain: float32 [2048], replicated, may hold values from 0.1 to 1.9
- w_qkv: bfloat16 [2048, 3, 2048], P(None, None, 'head'), may hold values from -0.125 to 0.125
- w_out: bfloat16 [2048, 2048], P('head'), may hold values from -0.125 to 0.125
- ffn_gain: float32 [2048], replicated, may hold values from 0.1 to 1.9
- routes: int32 [2048, 8], P(('tok', 'head')), may hold values from 0 to 15, all different within a row; in each aligned block of 64 rows (0 to 63, 64 to 127, ...) at most 64 rows name the same one
- route_weight: float32 [2048, 8], P(('tok', 'head')), may hold values from 0.1 to 1
- w_expert: bfloat16 [16, 3, 2048, 1024], P('tok', None, None, 'head'), may hold values from -0.125 to 0.125
Outputs:
- hidden_out: bfloat16 [2048, 2048], P(('tok', 'head'))
- new_cache_k: bfloat16 [16, 1024, 2048], P('tok', None, 'head')
- new_cache_v: bfloat16 [16, 1024, 2048], P('tok', None, 'head')
The draws below stay inside these ranges and needn't reach their ends.
Inputs may be any that keep to these rules, and one draw needn't show every extreme that they name: `token_req`: within each group of 256 consecutive tokens, the tokens of request 0 come first and those of request 1 follow; each request has at least one token. `cache_len`: A request's cache length plus its number of tokens is at most 1024. `routes`: each row names 8 different experts; in each aligned block of 64 rows (the rows of one device) no expert is named more than 64 times.
All inputs are finite; a program needn't handle non-finite values.
Results may differ from the reference program's by a relative error of at most 0.018.
Values may be sent and summed in bfloat16 or wider, within the bound.
A program may use at most 192 MiB of HBM per device.

```python
import math
import jax
import jax.numpy as jnp
import numpy as np
from jax import lax

D = 2048
H = 16
HD = 128
FF = 1024
TOPK = 8
TOK_DEV = 64
REQ_GRP = 2
CAP = 1024
WIN = 384
EXPERTS = 16
TOK_GRP = 256
TOKENS = 2048
REQS = 16
MOST = 64


def layout_parts(key):
    folded = jax.random.fold_in(key, 11)
    groups = TOKENS // TOK_GRP
    key_one, key_two, key_three, key_four, key_five = jax.random.split(folded, 5)
    single = jax.random.randint(key_one, (groups,), 0, 2).at[0].set(1)
    sizeable = jax.random.randint(key_two, (groups,), TOK_GRP // 4, TOK_GRP // 2 + 1)
    second_count = jnp.where(single == 1, 1, sizeable)
    first_count = TOK_GRP - second_count
    counts = jnp.stack([first_count, second_count], axis=1)
    position = jnp.arange(TOK_GRP, dtype=jnp.int32)
    request = (position[None, :] >= first_count[:, None]).astype(jnp.int32).reshape(-1)
    long_flag = jax.random.randint(key_three, (groups, 2), 0, 2).at[0, 0].set(1).at[0, 1].set(1).at[groups - 1, 0].set(0)
    offset = jax.random.randint(key_four, (groups, 2), 0, CAP // 16).at[0, 0].set(0).at[0, 1].set(0)
    short_len = jax.random.randint(key_five, (groups, 2), 16, CAP // 8).at[groups - 1, 0].set(16)
    lengths = jnp.where(long_flag == 1, CAP - counts - offset, short_len)
    return (request, lengths.reshape(-1).astype(jnp.int32))


def draw_token_req(key, part):
    return layout_parts(key)[0]


def draw_cache_len(key, part):
    return layout_parts(key)[1]


def draw_cache_k(key, part):
    full_shape = (REQS, CAP, H * HD)
    values = jax.random.normal(key, full_shape, jnp.float32) * 2.0
    return jnp.clip(values, -64.0, 64.0).astype(jnp.bfloat16)


def place_ends(result, key, least, largest):
    extent = result.shape
    index_at = [jax.random.randint(jax.random.fold_in(key, axis), (), 0, extent[axis]) for axis in range(len(extent))]
    result = result.at[tuple(index_at)].set(least)
    longest = extent.index(max(extent))
    index_at[longest] = (index_at[longest] + 1) % extent[longest]
    return result.at[tuple(index_at)].set(largest)


def block_levels(own_key, extent, cuts, least, high):
    level = 1.0
    for dim, shards_of in cuts:
        steps = jax.random.uniform(jax.random.fold_in(jax.random.fold_in(own_key, 6), dim), (shards_of,), jnp.float32, least / len(cuts), high / len(cuts))
        level = level * jnp.repeat(jnp.exp(steps), extent[dim] // shards_of).reshape((-1,) + (1,) * (len(extent) - 1 - dim))
    return level


def shared_out(key, own, number, rows, number_of, top, most, lean):
    sequence = jax.random.permutation(key, number_of)
    packed, usual = portions_of(number_of, rows * top, most, lean, True), portions_of(number_of, rows * top, most, lean, False)
    places = jnp.arange(number_of)

    def named(sizes, offset_by):
        used = int((sizes > 0).sum())
        fixed = max(1, used // 4)
        shifted = fixed + (places - fixed + offset_by * (used - fixed)) % max(1, number_of - fixed)
        return jnp.zeros((number_of,), jnp.int32).at[sequence[jnp.where(places < fixed, places, shifted)]].set(jnp.asarray(sizes, jnp.int32))

    sizes = jnp.where(number % 4 == 0, named(packed, number // 4), named(usual, number - number // 4 - 1))
    mixed = jax.random.permutation(jax.random.fold_in(own, 3), number_of)
    donor, taker = mixed[0:number_of // 2 * 2:2], mixed[1:number_of // 2 * 2:2]
    margin = jnp.minimum(sizes[donor] - 1, most - sizes[taker]) // 2
    margin = jnp.where((donor == sequence[0]) | (taker == sequence[0]) | (sizes[taker] == 0), 0, jnp.maximum(margin, 0))
    shifted = jax.random.randint(jax.random.fold_in(own, 4), (number_of // 2,), 0, 1 << 20) % (margin + 1)
    sizes = sizes.at[donor].add(-shifted).at[taker].add(shifted)
    items = jnp.searchsorted(jnp.cumsum(sizes), jnp.arange(rows * top), side="right").astype(jnp.int32)
    grid = items.reshape(top, rows).T
    grid = grid[jax.random.permutation(jax.random.fold_in(own, 1), rows)]
    offset_by = jax.random.randint(jax.random.fold_in(own, 2), (rows, 1), 0, top)
    return jnp.take_along_axis(grid, (jnp.arange(top)[None, :] + offset_by) % top, axis=1)


def portions_of(amount, total, most, skew, full):
    weights = [(1 << 20) // math.isqrt(rank ** skew) + 1 for rank in range(1, amount + 1)]
    largest = most if full else min(most, max(-(-total // amount), total * weights[0] // sum(weights)))
    least = 1 if total - largest >= amount - 1 else 0
    given, rest = [largest] + [least] * (amount - 1), total - largest - least * (amount - 1)
    while rest > 0:
        candidates = [i for i in range(1, amount) if given[i] < largest] or [i for i in range(1, amount) if given[i] < most]
        pool, budget = sum([weights[i] for i in candidates]), rest
        for i in candidates:
            extra = min(most - given[i], max(1, budget * weights[i] // pool), rest)
            given[i] = given[i] + extra
            rest = rest - extra
    return np.array(given)


def centred(key, dims, scale, most, pieces=(), kind=jnp.bfloat16):
    result = jax.random.normal(key, dims, jnp.float32) * scale
    if len(pieces) > 0:
        result = block_levels(key, dims, pieces, -0.22, 0.18) * result
    return jnp.clip(result, min=-most, max=most).astype(kind)


def setup_inputs(seed: int = 0) -> dict:
    splits = jax.random.split(jax.random.key(seed), 14)
    tokens = centred(splits[0], (TOKENS, D), 1.0, 6.0, ((0, 32),))
    token_req = draw_token_req(jax.random.fold_in(splits[13], 71), 0)
    cache_len = draw_cache_len(jax.random.fold_in(splits[13], 71), 0)
    sink_count = place_ends(jax.random.randint(splits[3], (REQS,), 1, 9), jax.random.fold_in(splits[3], 1), 1, 8).astype(jnp.int32)
    cache_k = draw_cache_k(jax.random.fold_in(splits[13], 71), 0)
    cache_v = centred(splits[5], (REQS, CAP, H * HD), 1.0, 6.0, ((0, 8), (2, 4)))
    attn_gain = jnp.clip(1.0 + 0.18 * jax.random.normal(splits[6], (D,), jnp.float32), 0.1, 1.9)
    w_qkv = centred(splits[7], (D, 3, H * HD), D ** -0.5, 0.125, ((2, 4),))
    w_out = centred(splits[8], (H * HD, D), (H * HD) ** -0.5, 0.125, ((0, 4),))
    ffn_gain = jnp.clip(1.0 + 0.18 * jax.random.normal(splits[9], (D,), jnp.float32), 0.1, 1.9)
    routes_keys = jax.random.split(jax.random.fold_in(splits[10], 1), TOKENS // TOK_DEV)
    routes_turns = jax.random.permutation(jax.random.fold_in(splits[10], 3), TOKENS // TOK_DEV)
    routes = jax.vmap(lambda own, number: shared_out(jax.random.fold_in(splits[10], 2), own, number, TOK_DEV, EXPERTS, TOPK, MOST, 2))(routes_keys, routes_turns).reshape((TOKENS, TOPK))
    route_weight = jnp.clip(jnp.exp(math.log(1.0) - 2.3025851 * jax.random.uniform(splits[11], (TOKENS, TOPK), jnp.float32) ** block_levels(splits[11], (TOKENS, TOPK), ((0, 32),), -0.2, 0.2)), 0.1, 1.0)
    w_expert = centred(splits[12], (EXPERTS, 3, D, FF), D ** -0.5, 0.125, ((0, 8), (3, 4)))
    return {"tokens": tokens, "token_req": token_req, "cache_len": cache_len, "sink_count": sink_count, "cache_k": cache_k, "cache_v": cache_v, "attn_gain": attn_gain, "w_qkv": w_qkv, "w_out": w_out, "ffn_gain": ffn_gain, "routes": routes, "route_weight": route_weight, "w_expert": w_expert}


norm_eps = 1e-05
rope_base = 50000.0

def rms_norm(values, gain_vec):
    widened = values.astype(jnp.float32)
    return widened * lax.rsqrt(lax.optimization_barrier(jnp.mean(widened * widened, axis=-1, keepdims=True)) + norm_eps) * gain_vec

def rotate(vectors, positions_all):
    half_width = vectors.shape[-1] // 2
    frequency = rope_base ** (-(jnp.arange(half_width, dtype=jnp.float32) * 2.0 / vectors.shape[-1]))
    angles = positions_all.astype(jnp.float32)[:, None] * frequency[None, :]
    cosine = jnp.cos(angles)[:, None, :]
    sine_part = jnp.sin(angles)[:, None, :]
    first_half = vectors[..., :half_width]
    second_half = vectors[..., half_width:]
    return jnp.concatenate([first_half * cosine - second_half * sine_part, second_half * cosine + first_half * sine_part], axis=-1)

def positions(request, lengths):
    one_hot = (request[:, None] == jnp.arange(REQ_GRP, dtype=jnp.int32)[None, :]).astype(jnp.int32)
    before = jnp.cumsum(one_hot, axis=0) - one_hot
    return lax.optimization_barrier(jnp.sum(one_hot * (before + lengths[None, :]), axis=1)).astype(jnp.int32)

def attend(query, keys_all, values_all, request, positions_all, sink_counts):
    scores = jnp.einsum('thd,rjhd->thrj', query.astype(jnp.float32), keys_all.astype(jnp.float32)) * HD ** (-0.5)
    slot_ids = jnp.arange(CAP, dtype=jnp.int32)
    same_req = jnp.arange(REQ_GRP, dtype=jnp.int32)[None, :, None] == request[:, None, None]
    causal = slot_ids[None, None, :] <= positions_all[:, None, None]
    window = (slot_ids[None, None, :] < sink_counts[None, :, None]) | (slot_ids[None, None, :] > positions_all[:, None, None] - WIN)
    allowed = (same_req & causal & window)[:, None]
    masked = jnp.where(allowed, scores, -1e+30)
    row_max = lax.optimization_barrier(jnp.max(masked, axis=(2, 3), keepdims=True))
    exp_scores = jnp.exp(masked - row_max)
    weights = (exp_scores / lax.optimization_barrier(jnp.sum(exp_scores, axis=(2, 3), keepdims=True))).astype(jnp.bfloat16)
    return jnp.einsum('thrj,rjhd->thd', weights.astype(jnp.float32), values_all.astype(jnp.float32)).astype(jnp.bfloat16)

def reference(tokens, token_req, cache_len, sink_count, cache_k, cache_v, attn_gain, w_qkv, w_out, ffn_gain, routes, route_weight, w_expert):
    groups = TOKENS // TOK_GRP
    normed = rms_norm(tokens, attn_gain).astype(jnp.bfloat16)
    projected = jnp.dot(normed, w_qkv.reshape(D, 3 * H * HD), preferred_element_type=jnp.float32).reshape(TOKENS, 3, H, HD)
    req_groups = token_req.reshape(groups, TOK_GRP)
    positions_all = jax.vmap(positions)(req_groups, cache_len.reshape(groups, REQ_GRP)).reshape(TOKENS)
    query = rotate(projected[:, 0], positions_all).astype(jnp.bfloat16)
    key_new = rotate(projected[:, 1], positions_all).astype(jnp.bfloat16).reshape(TOKENS, H * HD)
    value_new = projected[:, 2].astype(jnp.bfloat16).reshape(TOKENS, H * HD)
    owner_row = jnp.arange(TOKENS, dtype=jnp.int32) // TOK_GRP * REQ_GRP + token_req
    new_cache_k = cache_k.at[owner_row, positions_all].set(key_new)
    new_cache_v = cache_v.at[owner_row, positions_all].set(value_new)

    def one_group(group_args):
        group_query, group_keys, group_values, group_req, group_pos, group_sinks = group_args
        return attend(group_query, group_keys.reshape(REQ_GRP, CAP, H, HD), group_values.reshape(REQ_GRP, CAP, H, HD), group_req, group_pos, group_sinks)
    attended = lax.map(one_group, (query.reshape(groups, TOK_GRP, H, HD), new_cache_k.reshape(groups, REQ_GRP, CAP, H * HD), new_cache_v.reshape(groups, REQ_GRP, CAP, H * HD), req_groups, positions_all.reshape(groups, TOK_GRP), sink_count.reshape(groups, REQ_GRP)))
    attended = attended.reshape(TOKENS, H * HD)
    residual = (tokens.astype(jnp.float32) + jnp.dot(attended, w_out, preferred_element_type=jnp.float32)).astype(jnp.bfloat16)
    ffn_input = rms_norm(residual, ffn_gain).astype(jnp.bfloat16)
    device_count = TOKENS // TOK_DEV
    flat_expert = routes.reshape(-1).astype(jnp.int32)
    one_hot = (flat_expert[:, None] == jnp.arange(EXPERTS, dtype=jnp.int32)[None, :]).astype(jnp.int32)
    one_hot = one_hot.reshape(device_count, TOK_DEV * TOPK, EXPERTS)
    before = jnp.cumsum(one_hot, axis=1) - one_hot
    slot_index = lax.optimization_barrier(jnp.sum(before * one_hot, axis=2)).reshape(-1).astype(jnp.int32)
    row_ids = jnp.arange(TOKENS * TOPK, dtype=jnp.int32)
    device_of = row_ids // (TOK_DEV * TOPK)
    token_of = row_ids // TOPK
    slot_table = jnp.full((EXPERTS, device_count, MOST), TOKENS, jnp.int32).at[flat_expert, device_of, slot_index].set(token_of)
    padded = jnp.concatenate([ffn_input, jnp.zeros((1, D), jnp.bfloat16)], axis=0)

    def one_expert(expert_args):
        table_rows, weight_set = expert_args
        slot_rows = padded[table_rows]
        gate_part = jnp.dot(slot_rows, weight_set[0], preferred_element_type=jnp.float32)
        up_part = jnp.dot(slot_rows, weight_set[1], preferred_element_type=jnp.float32)
        hidden = (jax.nn.silu(gate_part) * up_part).astype(jnp.bfloat16)
        return lax.dot_general(hidden, weight_set[2], (((1,), (1,)), ((), ())), preferred_element_type=jnp.float32).astype(jnp.bfloat16)
    expert_out = lax.map(one_expert, (slot_table.reshape(EXPERTS, device_count * MOST), w_expert))
    picked = expert_out.reshape(-1, D)[flat_expert * (device_count * MOST) + device_of * MOST + slot_index]
    combined = lax.optimization_barrier(jnp.sum(route_weight.reshape(TOKENS, TOPK, 1) * picked.reshape(TOKENS, TOPK, D).astype(jnp.float32), axis=1))
    hidden_out = (residual.astype(jnp.float32) + combined).astype(jnp.bfloat16)
    return (hidden_out, new_cache_k, new_cache_v)
```

```python
import functools

import jax
import jax.numpy as jnp
import numpy as np
from jax import lax
from jax.experimental import pallas as pl
from jax.experimental.pallas import tpu as pltpu
from jax.sharding import PartitionSpec as P

HD = 128
REQ_GRP = 2
WIN = 384
HEADS_STEP = 2
PAD = 16
norm_eps = 1e-05
rope_base = 50000.0
LOG2E = 1.4426950408889634


def rms_norm(values, gain_vec):
    widened = values.astype(jnp.float32)
    return (
        widened
        * lax.rsqrt(jnp.mean(widened * widened, axis=-1, keepdims=True) + norm_eps)
        * gain_vec
    )


def rope_table(rows, before, after):
    half = HD // 2
    freq = np.float32(rope_base) ** (-(np.arange(half, dtype=np.float32) * np.float32(2.0) / np.float32(HD)))
    pos = np.arange(-before, after, dtype=np.float32)
    angle = (pos[:, None] * freq[None, :].astype(np.float32)).astype(np.float64)
    cos, sin = np.cos(angle), np.sin(angle)
    return (
        np.concatenate([cos, cos], axis=1).astype(np.float32),
        np.concatenate([-sin, sin], axis=1).astype(np.float32),
    )


def attn_kernel(rows_dev, cap, lens_ref, sinks_ref, x_ref, cos_ref, sin_ref, w_ref, ck_ref, cv_ref, wo_ref,
                nk_ref, nv_ref, out_ref, bias_ref, hot_ref, acc_ref):
    step = pl.program_id(0)
    parts, padded, width = x_ref.shape
    rows = parts * rows_dev
    slots = REQ_GRP * cap
    second = jnp.sum(x_ref[:, rows_dev:, :HD].astype(jnp.float32)).astype(jnp.int32)
    first = rows - second
    len0, len1 = lens_ref[0], lens_ref[1]
    sink0, sink1 = sinks_ref[0], sinks_ref[1]

    @pl.when(step == 0)
    def _():
        acc_ref[...] = jnp.zeros_like(acc_ref)
        tok = lax.broadcasted_iota(jnp.int32, (rows, cap), 0)
        slot = lax.broadcasted_iota(jnp.int32, (rows, cap), 1)
        for r, (base, sinks) in enumerate(((len0, sink0), (len1 - first, sink1))):
            pos = tok + base
            mine = (tok < first) if r == 0 else (tok >= first)
            ok = mine & (slot <= pos) & ((slot < sinks) | (slot > pos - WIN))
            bias_ref[:, r * cap:(r + 1) * cap] = jnp.where(ok, 0.0, -1e30)
        tok = lax.broadcasted_iota(jnp.int32, (cap, rows), 1)
        slot = lax.broadcasted_iota(jnp.int32, (cap, rows), 0)
        for r, base in enumerate((len0, len1 - first)):
            mine = (tok < first) if r == 0 else (tok >= first)
            hot = mine & (slot == tok + base)
            hot_ref[r * cap:(r + 1) * cap, :] = jnp.where(hot, 1.0, 0.0).astype(jnp.bfloat16)

    x = x_ref[:, :rows_dev, :].reshape(rows, width)
    tok = lax.broadcasted_iota(jnp.int32, (rows, HD), 0)
    early = tok < first
    cos = jnp.where(early, cos_ref[pl.ds(len0 + rows, rows), :], cos_ref[pl.ds(len1 - first + rows, rows), :])
    sin = jnp.where(early, sin_ref[pl.ds(len0 + rows, rows), :], sin_ref[pl.ds(len1 - first + rows, rows), :])

    def rotated(v):
        cols = []
        for h in range(HEADS_STEP):
            part = v[:, h * HD:(h + 1) * HD]
            cols.append((part * cos + pltpu.roll(part, HD // 2, 1) * sin).astype(jnp.bfloat16))
        return cols

    q = rotated(jnp.dot(x, w_ref[0], preferred_element_type=jnp.float32))
    k = jnp.concatenate(rotated(jnp.dot(x, w_ref[1], preferred_element_type=jnp.float32)), axis=1)
    v = jnp.dot(x, w_ref[2], preferred_element_type=jnp.float32).astype(jnp.bfloat16)

    for r, (start, count) in enumerate(((len0, first), (len1, second))):
        span = slice(r * cap, (r + 1) * cap)
        slot = lax.broadcasted_iota(jnp.int32, (cap, HEADS_STEP * HD), 0)
        written = (slot >= start) & (slot < start + count)
        hot = hot_ref[span, :]
        new_k = jnp.dot(hot, k, preferred_element_type=jnp.float32)
        nk_ref[span, :] = jnp.where(written, new_k, ck_ref[span, :].astype(jnp.float32)).astype(jnp.bfloat16)
        new_v = jnp.dot(hot, v, preferred_element_type=jnp.float32)
        nv_ref[span, :] = jnp.where(written, new_v, cv_ref[span, :].astype(jnp.float32)).astype(jnp.bfloat16)

    mixed = []
    for h in range(HEADS_STEP):
        cols = slice(h * HD, (h + 1) * HD)
        scores = lax.dot_general(q[h], nk_ref[:, cols], (((1,), (1,)), ((), ())), preferred_element_type=jnp.float32)
        scores = scores * (HD ** (-0.5) * LOG2E) + bias_ref[...]
        top = jnp.max(scores, axis=1, keepdims=True)
        weights = jnp.exp2(scores - top)
        total = jnp.sum(weights, axis=1, keepdims=True)
        part = jnp.dot(weights.astype(jnp.bfloat16), nv_ref[:, cols], preferred_element_type=jnp.float32)
        mixed.append((part / total).astype(jnp.bfloat16))
    acc_ref[...] += jnp.dot(jnp.concatenate(mixed, axis=1), wo_ref[...], preferred_element_type=jnp.float32)

    @pl.when(step == pl.num_programs(0) - 1)
    def _():
        out_ref[...] = acc_ref[...].astype(jnp.bfloat16)


def attention(gathered, rows_dev, lens, sinks, cache_k, cache_v, w_qkv, w_out):
    parts, padded, width = gathered.shape
    rows = parts * rows_dev
    reqs, cap, cols = cache_k.shape
    slots = reqs * cap
    step_cols = HEADS_STEP * HD
    cos, sin = rope_table(rows, rows, cap + rows)
    smem = pl.BlockSpec(memory_space=pltpu.SMEM)
    full2 = lambda s: (0, 0)
    nk, nv, out = pl.pallas_call(
        functools.partial(attn_kernel, rows_dev, cap),
        grid=(cols // step_cols,),
        in_specs=[
            smem,
            smem,
            pl.BlockSpec(gathered.shape, lambda s: (0, 0, 0)),
            pl.BlockSpec(cos.shape, full2),
            pl.BlockSpec(sin.shape, full2),
            pl.BlockSpec((3, width, step_cols), lambda s: (0, 0, s)),
            pl.BlockSpec((slots, step_cols), lambda s: (0, s)),
            pl.BlockSpec((slots, step_cols), lambda s: (0, s)),
            pl.BlockSpec((step_cols, width), lambda s: (s, 0)),
        ],
        out_specs=[
            pl.BlockSpec((slots, step_cols), lambda s: (0, s)),
            pl.BlockSpec((slots, step_cols), lambda s: (0, s)),
            pl.BlockSpec((rows, width), full2),
        ],
        out_shape=[
            jax.ShapeDtypeStruct((slots, cols), jnp.bfloat16),
            jax.ShapeDtypeStruct((slots, cols), jnp.bfloat16),
            jax.ShapeDtypeStruct((rows, width), jnp.bfloat16),
        ],
        scratch_shapes=[
            pltpu.VMEM((rows, slots), jnp.float32),
            pltpu.VMEM((slots, rows), jnp.bfloat16),
            pltpu.VMEM((rows, width), jnp.float32),
        ],
        compiler_params=pltpu.CompilerParams(vmem_limit_bytes=56 * 2**20),
        name="attention",
    )(
        lens,
        sinks,
        gathered,
        cos,
        sin,
        jnp.transpose(w_qkv, (1, 0, 2)),
        cache_k.reshape(slots, cols),
        cache_v.reshape(slots, cols),
        w_out,
    )
    return nk.reshape(cache_k.shape), nv.reshape(cache_v.shape), out


def expert_kernel(x_ref, gate_ref, w_ref, out_ref):
    x = x_ref[...]
    total = None
    for e in range(w_ref.shape[0]):
        g = jnp.dot(x, w_ref[e, 0], preferred_element_type=jnp.float32)
        u = jnp.dot(x, w_ref[e, 1], preferred_element_type=jnp.float32)
        act = (g / (1.0 + jnp.exp(-g)) * u * gate_ref[:, e:e + 1]).astype(jnp.bfloat16)
        part = lax.dot_general(act, w_ref[e, 2], (((1,), (1,)), ((), ())), preferred_element_type=jnp.float32)
        total = part if total is None else total + part
    out_ref[...] = total.astype(jnp.bfloat16)


def experts(rows, gates, w_expert):
    count, width = rows.shape
    block = 256
    n_exp = w_expert.shape[0]
    return pl.pallas_call(
        expert_kernel,
        grid=(count // block,),
        in_specs=[
            pl.BlockSpec((block, width), lambda i: (i, 0)),
            pl.BlockSpec((block, n_exp), lambda i: (i, 0)),
            pl.BlockSpec(w_expert.shape, lambda i: (0, 0, 0, 0)),
        ],
        out_specs=pl.BlockSpec((block, width), lambda i: (i, 0)),
        out_shape=jax.ShapeDtypeStruct((count, width), jnp.bfloat16),
        compiler_params=pltpu.CompilerParams(vmem_limit_bytes=56 * 2**20),
        name="experts",
    )(rows, gates, w_expert)


def on_device(
    tokens,
    token_req,
    cache_len,
    sink_count,
    cache_k,
    cache_v,
    attn_gain,
    w_qkv,
    w_out,
    ffn_gain,
    routes,
    route_weight,
    w_expert,
):
    tok_dev, width = tokens.shape
    exp_dev = w_expert.shape[0]
    expert_total = exp_dev * lax.axis_size("tok")
    normed = rms_norm(tokens, attn_gain).astype(jnp.bfloat16)
    marks = jnp.zeros((PAD, width), jnp.bfloat16).at[0, :tok_dev].set(token_req.astype(jnp.bfloat16))
    sent = jnp.concatenate([normed, marks], axis=0)
    gathered = lax.all_gather(sent, "head", axis=0)
    chosen = routes[:, :, None] == jnp.arange(expert_total, dtype=jnp.int32)[None, None, :]
    gates = jnp.sum(jnp.where(chosen, route_weight[:, :, None], 0.0), axis=1)
    gates = lax.all_gather(gates, ("tok", "head"), axis=0, tiled=True)
    gates = lax.dynamic_slice_in_dim(gates, lax.axis_index("tok") * exp_dev, exp_dev, axis=1)
    new_k, new_v, mixed = attention(gathered, tok_dev, cache_len, sink_count, cache_k, cache_v, w_qkv, w_out)
    mixed = lax.psum_scatter(mixed, "head", scatter_dimension=0, tiled=True)
    residual = (tokens.astype(jnp.float32) + mixed.astype(jnp.float32)).astype(jnp.bfloat16)
    ffn_input = rms_norm(residual, ffn_gain).astype(jnp.bfloat16)
    rows = lax.all_gather(ffn_input, ("tok", "head"), axis=0, tiled=True)
    partial = experts(rows, gates, w_expert)
    combined = lax.psum_scatter(partial, ("tok", "head"), scatter_dimension=0, tiled=True)
    hidden_out = (residual.astype(jnp.float32) + combined.astype(jnp.float32)).astype(jnp.bfloat16)
    return (hidden_out, new_k, new_v)


def solution(mesh):
    return jax.shard_map(
        on_device,
        mesh=mesh,
        in_specs=(
            P(("tok", "head"), None),
            P(("tok", "head")),
            P("tok"),
            P("tok"),
            P("tok", None, "head"),
            P("tok", None, "head"),
            P(),
            P(None, None, "head"),
            P("head", None),
            P(),
            P(("tok", "head"), None),
            P(("tok", "head"), None),
            P("tok", None, None, "head"),
        ),
        out_specs=(P(("tok", "head"), None), P("tok", None, "head"), P("tok", None, "head")),
        check_vma=False,
    )
```

```python
import functools

import jax
import jax.numpy as jnp
import numpy as np
from jax import lax
from jax.experimental import pallas as pl
from jax.experimental.pallas import tpu as pltpu
from jax.sharding import PartitionSpec as P

HD = 128
REQ_GRP = 2
WIN = 384
HEADS_STEP = 2
PAD = 16
norm_eps = 1e-05
rope_base = 50000.0
LOG2E = 1.4426950408889634


def rms_norm(values, gain_vec):
    widened = values.astype(jnp.float32)
    return (
        widened
        * lax.rsqrt(jnp.mean(widened * widened, axis=-1, keepdims=True) + norm_eps)
        * gain_vec
    )


def rope_table(rows, before, after):
    half = HD // 2
    freq = np.float32(rope_base) ** (-(np.arange(half, dtype=np.float32) * np.float32(2.0) / np.float32(HD)))
    pos = np.arange(-before, after, dtype=np.float32)
    angle = (pos[:, None] * freq[None, :].astype(np.float32)).astype(np.float64)
    cos, sin = np.cos(angle), np.sin(angle)
    return (
        np.concatenate([cos, cos], axis=1).astype(np.float32),
        np.concatenate([-sin, sin], axis=1).astype(np.float32),
    )


def attn_kernel(rows_dev, cap, lens_ref, sinks_ref, x_ref, cos_ref, sin_ref, w_ref, ck_ref, cv_ref, wo_ref,
                nk_ref, nv_ref, out_ref, bias_ref, hot_ref, acc_ref):
    step = pl.program_id(0)
    parts, padded, width = x_ref.shape
    rows = parts * rows_dev
    slots = REQ_GRP * cap
    second = jnp.sum(x_ref[:, rows_dev:, :HD].astype(jnp.float32)).astype(jnp.int32)
    first = rows - second
    len0, len1 = lens_ref[0], lens_ref[1]
    sink0, sink1 = sinks_ref[0], sinks_ref[1]

    @pl.when(step == 0)
    def _():
        acc_ref[...] = jnp.zeros_like(acc_ref)
        tok = lax.broadcasted_iota(jnp.int32, (rows, cap), 0)
        slot = lax.broadcasted_iota(jnp.int32, (rows, cap), 1)
        for r, (base, sinks) in enumerate(((len0, sink0), (len1 - first, sink1))):
            pos = tok + base
            mine = (tok < first) if r == 0 else (tok >= first)
            ok = mine & (slot <= pos) & ((slot < sinks) | (slot > pos - WIN))
            bias_ref[:, r * cap:(r + 1) * cap] = jnp.where(ok, 0.0, -1e30)
        tok = lax.broadcasted_iota(jnp.int32, (cap, rows), 1)
        slot = lax.broadcasted_iota(jnp.int32, (cap, rows), 0)
        for r, base in enumerate((len0, len1 - first)):
            mine = (tok < first) if r == 0 else (tok >= first)
            hot = mine & (slot == tok + base)
            hot_ref[r * cap:(r + 1) * cap, :] = jnp.where(hot, 1.0, 0.0).astype(jnp.bfloat16)

    x = x_ref[:, :rows_dev, :].reshape(rows, width)
    tok = lax.broadcasted_iota(jnp.int32, (rows, HD), 0)
    early = tok < first
    cos = jnp.where(early, cos_ref[pl.ds(len0 + rows, rows), :], cos_ref[pl.ds(len1 - first + rows, rows), :])
    sin = jnp.where(early, sin_ref[pl.ds(len0 + rows, rows), :], sin_ref[pl.ds(len1 - first + rows, rows), :])

    def rotated(v):
        cols = []
        for h in range(HEADS_STEP):
            part = v[:, h * HD:(h + 1) * HD]
            cols.append((part * cos + pltpu.roll(part, HD // 2, 1) * sin).astype(jnp.bfloat16))
        return cols

    q = rotated(jnp.dot(x, w_ref[0], preferred_element_type=jnp.float32))
    k = jnp.concatenate(rotated(jnp.dot(x, w_ref[1], preferred_element_type=jnp.float32)), axis=1)
    v = jnp.dot(x, w_ref[2], preferred_element_type=jnp.float32).astype(jnp.bfloat16)

    for r, (start, count) in enumerate(((len0, first), (len1, second))):
        span = slice(r * cap, (r + 1) * cap)
        slot = lax.broadcasted_iota(jnp.int32, (cap, HEADS_STEP * HD), 0)
        written = (slot >= start) & (slot < start + count)
        hot = hot_ref[span, :]
        new_k = jnp.dot(hot, k, preferred_element_type=jnp.float32)
        nk_ref[span, :] = jnp.where(written, new_k, ck_ref[span, :].astype(jnp.float32)).astype(jnp.bfloat16)
        new_v = jnp.dot(hot, v, preferred_element_type=jnp.float32)
        nv_ref[span, :] = jnp.where(written, new_v, cv_ref[span, :].astype(jnp.float32)).astype(jnp.bfloat16)

    mixed = []
    for h in range(HEADS_STEP):
        cols = slice(h * HD, (h + 1) * HD)
        scores = lax.dot_general(q[h], nk_ref[:, cols], (((1,), (1,)), ((), ())), preferred_element_type=jnp.float32)
        scores = scores * (HD ** (-0.5) * LOG2E) + bias_ref[...]
        top = jnp.max(scores, axis=1, keepdims=True)
        weights = jnp.exp2(scores - top)
        total = jnp.sum(weights, axis=1, keepdims=True)
        part = jnp.dot(weights.astype(jnp.bfloat16), nv_ref[:, cols], preferred_element_type=jnp.float32)
        mixed.append((part / total).astype(jnp.bfloat16))
    acc_ref[...] += jnp.dot(jnp.concatenate(mixed, axis=1), wo_ref[...], preferred_element_type=jnp.float32)

    @pl.when(step == pl.num_programs(0) - 1)
    def _():
        out_ref[...] = acc_ref[...].astype(jnp.bfloat16)


def attention(gathered, rows_dev, lens, sinks, cache_k, cache_v, w_qkv, w_out):
    parts, padded, width = gathered.shape
    rows = parts * rows_dev
    reqs, cap, cols = cache_k.shape
    slots = reqs * cap
    step_cols = HEADS_STEP * HD
    cos, sin = rope_table(rows, rows, cap + rows)
    smem = pl.BlockSpec(memory_space=pltpu.SMEM)
    full2 = lambda s: (0, 0)
    nk, nv, out = pl.pallas_call(
        functools.partial(attn_kernel, rows_dev, cap),
        grid=(cols // step_cols,),
        in_specs=[
            smem,
            smem,
            pl.BlockSpec(gathered.shape, lambda s: (0, 0, 0)),
            pl.BlockSpec(cos.shape, full2),
            pl.BlockSpec(sin.shape, full2),
            pl.BlockSpec((3, width, step_cols), lambda s: (0, 0, s)),
            pl.BlockSpec((slots, step_cols), lambda s: (0, s)),
            pl.BlockSpec((slots, step_cols), lambda s: (0, s)),
            pl.BlockSpec((step_cols, width), lambda s: (s, 0)),
        ],
        out_specs=[
            pl.BlockSpec((slots, step_cols), lambda s: (0, s)),
            pl.BlockSpec((slots, step_cols), lambda s: (0, s)),
            pl.BlockSpec((rows, width), full2),
        ],
        out_shape=[
            jax.ShapeDtypeStruct((slots, cols), jnp.bfloat16),
            jax.ShapeDtypeStruct((slots, cols), jnp.bfloat16),
            jax.ShapeDtypeStruct((rows, width), jnp.bfloat16),
        ],
        scratch_shapes=[
            pltpu.VMEM((rows, slots), jnp.float32),
            pltpu.VMEM((slots, rows), jnp.bfloat16),
            pltpu.VMEM((rows, width), jnp.float32),
        ],
        compiler_params=pltpu.CompilerParams(vmem_limit_bytes=56 * 2**20),
        name="attention",
    )(
        lens,
        sinks,
        gathered,
        cos,
        sin,
        jnp.transpose(w_qkv, (1, 0, 2)),
        cache_k.reshape(slots, cols),
        cache_v.reshape(slots, cols),
        w_out,
    )
    return nk.reshape(cache_k.shape), nv.reshape(cache_v.shape), out


def expert_kernel(x_ref, gate_ref, w_ref, out_ref):
    x = x_ref[...]
    total = None
    for e in range(w_ref.shape[0]):
        g = jnp.dot(x, w_ref[e, 0], preferred_element_type=jnp.float32)
        u = jnp.dot(x, w_ref[e, 1], preferred_element_type=jnp.float32)
        act = (g / (1.0 + jnp.exp(-g)) * u * gate_ref[:, e:e + 1]).astype(jnp.bfloat16)
        part = lax.dot_general(act, w_ref[e, 2], (((1,), (1,)), ((), ())), preferred_element_type=jnp.float32)
        total = part if total is None else total + part
    out_ref[...] = total.astype(jnp.bfloat16)


def experts(rows, gates, w_expert):
    count, width = rows.shape
    block = 256
    n_exp = w_expert.shape[0]
    return pl.pallas_call(
        expert_kernel,
        grid=(count // block,),
        in_specs=[
            pl.BlockSpec((block, width), lambda i: (i, 0)),
            pl.BlockSpec((block, n_exp), lambda i: (i, 0)),
            pl.BlockSpec(w_expert.shape, lambda i: (0, 0, 0, 0)),
        ],
        out_specs=pl.BlockSpec((block, width), lambda i: (i, 0)),
        out_shape=jax.ShapeDtypeStruct((count, width), jnp.bfloat16),
        compiler_params=pltpu.CompilerParams(vmem_limit_bytes=56 * 2**20),
        name="experts",
    )(rows, gates, w_expert)


MESH = pl.DeviceIdType.MESH
VMEM_LIMIT = 60 * 2**20


def partners():
    head, tok = lax.axis_index("head"), lax.axis_index("tok")
    z, core = tok // 2, tok % 2
    across = [head + 1 - 2 * (head % 2), (head + 2) % 4, 3 - head]
    layer = [{"head": h, "tok": tok} for h in across]
    sibling = {"head": head, "tok": 2 * z + 1 - core}
    column = [{"head": head, "tok": ((z + d) % 4) * 2 + core} for d in range(4)]
    return head, across, layer, sibling, column


def greet(devices):
    barrier = pltpu.get_barrier_semaphore()
    for device in devices:
        pl.semaphore_signal(barrier, inc=1, device_id=device, device_id_type=MESH)
    pl.semaphore_wait(barrier, len(devices))


def head_gather_kernel(tokens_ref, gain_ref, marks_ref, out_ref, send_sem, recv_sem):
    head, across, layer, _, _ = partners()
    rows_dev = tokens_ref.shape[0]
    rows = out_ref.shape[1]
    cut = rows // 2 // 16 * 16

    def copy(index, src, dst, device):
        return pltpu.make_async_remote_copy(
            src_ref=src, dst_ref=dst, send_sem=send_sem.at[index], recv_sem=recv_sem.at[index],
            device_id=device, device_id_type=MESH)

    out_ref[head, :rows_dev, :] = rms_norm(tokens_ref[...], gain_ref[...]).astype(jnp.bfloat16)
    out_ref[head, rows_dev:, :] = marks_ref[...]
    greet(layer[:2])
    own = out_ref.at[head]
    first = [copy(i, own, own, layer[i]) for i in range(2)]
    for c in first:
        c.start()
    arrived = [copy(i, out_ref.at[across[i]], out_ref.at[across[i]], layer[i]) for i in range(2)]
    spans = [pl.ds(0, cut), pl.ds(cut, rows - cut)]
    later = []
    for i in range(2):
        arrived[i].wait_recv()
        block = out_ref.at[across[i], spans[i]]
        later.append(copy(2 + i, block, block, layer[1 - i]))
        later[i].start()
    for i in range(2):
        block = out_ref.at[across[2], spans[i]]
        copy(2 + i, block, block, layer[1 - i]).wait_recv()
    for c in first + later:
        c.wait_send()


def head_gather(tokens, gain, marks, parts):
    rows = tokens.shape[0] + marks.shape[0]
    vmem = pl.BlockSpec(memory_space=pltpu.VMEM)
    return pl.pallas_call(
        head_gather_kernel,
        in_specs=[vmem] * 3,
        out_specs=vmem,
        out_shape=jax.ShapeDtypeStruct((parts, rows, tokens.shape[1]), jnp.bfloat16),
        scratch_shapes=[pltpu.SemaphoreType.DMA((4,)), pltpu.SemaphoreType.DMA((4,))],
        compiler_params=pltpu.CompilerParams(collective_id=0, has_side_effects=True, vmem_limit_bytes=VMEM_LIMIT),
        name="head_gather",
    )(tokens, gain.reshape(1, -1), marks)


def layer_kernel(mixed_ref, tokens_ref, gain_ref, gates_ref, w_ref, out_ref,
                 head_buf, resid, x_buf, part, core_buf, diag_buf, side_buf, z_buf, send_sem, recv_sem):
    head, across, layer, sibling, column = partners()
    tok = lax.axis_index("tok")
    rows, width = tokens_ref.shape
    n_exp = w_ref.shape[0]
    half = rows // 2
    started = []

    def copy(index, src, dst, device):
        return pltpu.make_async_remote_copy(
            src_ref=src, dst_ref=dst, send_sem=send_sem.at[index], recv_sem=recv_sem.at[index],
            device_id=device, device_id_type=MESH)

    def start(*args):
        c = copy(*args)
        c.start()
        started.append(c)

    def arrived(index, dst, device):
        copy(index, dst, dst, device).wait_recv()

    greet(layer + [sibling] + column[1:])

    for r in (2, 0, 1):
        start(r, mixed_ref.at[across[r]], head_buf.at[r], layer[r])
    total = tokens_ref[...].astype(jnp.float32)
    mine = mixed_ref[head].astype(jnp.float32)
    for r in range(3):
        arrived(r, head_buf.at[r], layer[r])
        mine = mine + head_buf[r].astype(jnp.float32)
    residual = (total + mine).astype(jnp.bfloat16)
    resid[...] = residual
    x_buf[0, 0, 0, :, :width] = rms_norm(residual, gain_ref[...]).astype(jnp.bfloat16)
    x_buf[0, 0, 0, :, width:] = gates_ref[...]

    low, high = pl.ds(0, half), pl.ds(half, half)

    def stage_a(s):
        if s:
            arrived(2 + s, x_buf.at[0, s, 0], column[4 - s])
        block = x_buf.at[0, s, 0]
        start(6 + s, block, x_buf.at[0, s, 1], layer[0])
        start(10 + s, block, x_buf.at[0, s, 2], layer[1])

    def stage_b(s):
        arrived(6 + s, x_buf.at[0, s, 1], layer[0])
        start(14 + s, x_buf.at[0, s, 1, low], x_buf.at[0, s, 3, low], layer[1])
        arrived(10 + s, x_buf.at[0, s, 2], layer[1])
        start(18 + s, x_buf.at[0, s, 2, high], x_buf.at[0, s, 3, high], layer[0])

    def stage_c(s):
        arrived(14 + s, x_buf.at[0, s, 3, low], layer[1])
        arrived(18 + s, x_buf.at[0, s, 3, high], layer[0])
        start(22 + s, x_buf.at[0, s], x_buf.at[1, s], sibling)

    def compute(index, s):
        x = x_buf[index, s, :, :, :width].reshape(4 * rows, width)
        gates = x_buf[index, s, :, :, width:].reshape(4 * rows, HD).astype(jnp.float32)
        lane = lax.broadcasted_iota(jnp.int32, gates.shape, 1) % (HD // 2)
        total = None
        for e in range(n_exp):
            gate = jnp.sum(jnp.where(lane == tok * n_exp + e, gates, 0.0), axis=1, keepdims=True)
            g = jnp.dot(x, w_ref[e, 0], preferred_element_type=jnp.float32)
            u = jnp.dot(x, w_ref[e, 1], preferred_element_type=jnp.float32)
            act = (g / (1.0 + jnp.exp(-g)) * u * gate).astype(jnp.bfloat16)
            p = lax.dot_general(act, w_ref[e, 2], (((1,), (1,)), ((), ())), preferred_element_type=jnp.float32)
            total = p if total is None else total + p
        part[index, s] = total.astype(jnp.bfloat16).reshape(4, rows, width)

    def stage_d(s):
        compute(0, s)
        arrived(22 + s, x_buf.at[1, s], sibling)
        compute(1, s)
        start(26 + s, part.at[1, s], core_buf.at[s], sibling)

    def add(r, s, other, span=slice(None)):
        part[0, s, r, span, :] = (part[0, s, r, span, :].astype(jnp.float32) + other.astype(jnp.float32)).astype(jnp.bfloat16)

    def stage_e(s):
        arrived(26 + s, core_buf.at[s], sibling)
        add(3, s, core_buf[s, 3])
        start(30 + s, part.at[0, s, 3, low], diag_buf.at[0, s], layer[0])
        start(34 + s, part.at[0, s, 3, high], diag_buf.at[1, s], layer[1])
        for r in range(3):
            add(r, s, core_buf[s, r])

    def stage_f(s):
        arrived(30 + s, diag_buf.at[0, s], layer[0])
        add(2, s, diag_buf[0, s], slice(0, half))
        start(42 + s, part.at[0, s, 2], side_buf.at[1, s], layer[1])
        arrived(34 + s, diag_buf.at[1, s], layer[1])
        add(1, s, diag_buf[1, s], slice(half, rows))
        start(38 + s, part.at[0, s, 1], side_buf.at[0, s], layer[0])

    def stage_g(s):
        arrived(38 + s, side_buf.at[0, s], layer[0])
        arrived(42 + s, side_buf.at[1, s], layer[1])
        add(0, s, side_buf[0, s].astype(jnp.float32) + side_buf[1, s].astype(jnp.float32))
        if s:
            start(45 + s, part.at[0, s, 0], z_buf.at[s - 1], column[4 - s])

    for s in (1, 3, 2):
        start(2 + s, x_buf.at[0, 0, 0], x_buf.at[0, s, 0], column[s])
    a, b, c, d, e, f, g = stage_a, stage_b, stage_c, stage_d, stage_e, stage_f, stage_g
    plan = (
        (a, 0), (a, 1), (b, 0), (c, 0), (d, 0),
        (a, 3), (b, 1), (c, 1), (e, 0), (d, 1),
        (a, 2), (b, 3), (c, 3), (f, 0), (e, 1), (d, 3),
        (b, 2), (c, 2), (g, 0), (f, 1), (e, 3), (d, 2),
        (g, 1), (f, 3), (e, 2), (g, 3), (f, 2), (g, 2),
    )
    for stage, s in plan:
        stage(s)

    total = part[0, 0, 0].astype(jnp.float32)
    for s in (1, 3, 2):
        arrived(45 + s, z_buf.at[s - 1], column[s])
        total = total + z_buf[s - 1].astype(jnp.float32)
    out_ref[...] = (resid[...].astype(jnp.float32) + total).astype(jnp.bfloat16)
    for c in started:
        c.wait_send()


def layer_rest(mixed, tokens, gain, gates, w_expert):
    rows, width = tokens.shape
    vmem = pl.BlockSpec(memory_space=pltpu.VMEM)
    bf16 = jnp.bfloat16
    return pl.pallas_call(
        layer_kernel,
        in_specs=[vmem] * 5,
        out_specs=vmem,
        out_shape=jax.ShapeDtypeStruct((rows, width), bf16),
        scratch_shapes=[
            pltpu.VMEM((3, rows, width), bf16),
            pltpu.VMEM((rows, width), bf16),
            pltpu.VMEM((2, 4, 4, rows, width + HD), bf16),
            pltpu.VMEM((2, 4, 4, rows, width), bf16),
            pltpu.VMEM((4, 4, rows, width), bf16),
            pltpu.VMEM((2, 4, rows // 2, width), bf16),
            pltpu.VMEM((2, 4, rows, width), bf16),
            pltpu.VMEM((3, rows, width), bf16),
            pltpu.SemaphoreType.DMA((49,)),
            pltpu.SemaphoreType.DMA((49,)),
        ],
        compiler_params=pltpu.CompilerParams(collective_id=1, has_side_effects=True, vmem_limit_bytes=VMEM_LIMIT),
        name="layer_rest",
    )(mixed.reshape(-1, rows, width), tokens, gain.reshape(1, -1), gates, w_expert)


def on_device(
    tokens,
    token_req,
    cache_len,
    sink_count,
    cache_k,
    cache_v,
    attn_gain,
    w_qkv,
    w_out,
    ffn_gain,
    routes,
    route_weight,
    w_expert,
):
    tok_dev, width = tokens.shape
    exp_dev = w_expert.shape[0]
    expert_total = exp_dev * lax.axis_size("tok")
    direct = lax.axis_size("tok") == 8 and lax.axis_size("head") == 4
    marks = jnp.zeros((PAD, width), jnp.bfloat16).at[0, :tok_dev].set(token_req.astype(jnp.bfloat16))
    chosen = routes[:, :, None] == jnp.arange(expert_total, dtype=jnp.int32)[None, None, :]
    gates = jnp.sum(jnp.where(chosen, route_weight[:, :, None], 0.0), axis=1)
    if direct:
        gathered = head_gather(tokens, attn_gain, marks, lax.axis_size("head"))
    else:
        normed = rms_norm(tokens, attn_gain).astype(jnp.bfloat16)
        gathered = lax.all_gather(jnp.concatenate([normed, marks], axis=0), "head", axis=0)
    new_k, new_v, mixed = attention(gathered, tok_dev, cache_len, sink_count, cache_k, cache_v, w_qkv, w_out)
    if direct:
        gates = jnp.pad(gates, ((0, 0), (0, HD // 2 - expert_total)))
        rounded = lax.reduce_precision(gates, 8, 7)
        sent = jnp.concatenate([rounded, gates - rounded], axis=1).astype(jnp.bfloat16)
        return (layer_rest(mixed, tokens, ffn_gain, sent, w_expert), new_k, new_v)
    gates = lax.all_gather(gates, ("tok", "head"), axis=0, tiled=True)
    gates = lax.dynamic_slice_in_dim(gates, lax.axis_index("tok") * exp_dev, exp_dev, axis=1)
    mixed = lax.psum_scatter(mixed, "head", scatter_dimension=0, tiled=True)
    residual = (tokens.astype(jnp.float32) + mixed.astype(jnp.float32)).astype(jnp.bfloat16)
    ffn_input = rms_norm(residual, ffn_gain).astype(jnp.bfloat16)
    rows = lax.all_gather(ffn_input, ("tok", "head"), axis=0, tiled=True)
    partial = experts(rows, gates, w_expert)
    combined = lax.psum_scatter(partial, ("tok", "head"), scatter_dimension=0, tiled=True)
    hidden_out = (residual.astype(jnp.float32) + combined.astype(jnp.float32)).astype(jnp.bfloat16)
    return (hidden_out, new_k, new_v)


def solution(mesh):
    return jax.shard_map(
        on_device,
        mesh=mesh,
        in_specs=(
            P(("tok", "head"), None),
            P(("tok", "head")),
            P("tok"),
            P("tok"),
            P("tok", None, "head"),
            P("tok", None, "head"),
            P(),
            P(None, None, "head"),
            P("head", None),
            P(),
            P(("tok", "head"), None),
            P(("tok", "head"), None),
            P("tok", None, None, "head"),
        ),
        out_specs=(P(("tok", "head"), None), P("tok", None, "head"), P("tok", None, "head")),
        check_vma=False,
    )
```

```python
import functools

import jax
import jax.numpy as jnp
import numpy as np
from jax import lax
from jax.experimental import pallas as pl
from jax.experimental.pallas import tpu as pltpu
from jax.sharding import PartitionSpec as P

HD = 128
REQ_GRP = 2
WIN = 384
HEADS_STEP = 2
PAD = 16
norm_eps = 1e-05
rope_base = 50000.0
LOG2E = 1.4426950408889634


def rms_norm(values, gain_vec):
    widened = values.astype(jnp.float32)
    return (
        widened
        * lax.rsqrt(jnp.mean(widened * widened, axis=-1, keepdims=True) + norm_eps)
        * gain_vec
    )


def rope_table(rows, before, after):
    half = HD // 2
    freq = np.float32(rope_base) ** (-(np.arange(half, dtype=np.float32) * np.float32(2.0) / np.float32(HD)))
    pos = np.arange(-before, after, dtype=np.float32)
    angle = (pos[:, None] * freq[None, :].astype(np.float32)).astype(np.float64)
    cos, sin = np.cos(angle), np.sin(angle)
    return (
        np.concatenate([cos, cos], axis=1).astype(np.float32),
        np.concatenate([-sin, sin], axis=1).astype(np.float32),
    )


def attn_kernel(rows_dev, cap, lens_ref, sinks_ref, x_ref, marks_ref, cos_ref, sin_ref, w_ref, ck_ref, cv_ref, wo_ref,
                nk_ref, nv_ref, out_ref, bias_ref, hot_ref, acc_ref):
    step = pl.program_id(0)
    parts, _, width = x_ref.shape
    rows = parts * rows_dev
    slots = REQ_GRP * cap
    second = jnp.sum(marks_ref[...].astype(jnp.float32)).astype(jnp.int32)
    first = rows - second
    len0, len1 = lens_ref[0], lens_ref[1]
    sink0, sink1 = sinks_ref[0], sinks_ref[1]

    @pl.when(step == 0)
    def _():
        acc_ref[...] = jnp.zeros_like(acc_ref)
        tok = lax.broadcasted_iota(jnp.int32, (rows, cap), 0)
        slot = lax.broadcasted_iota(jnp.int32, (rows, cap), 1)
        for r, (base, sinks) in enumerate(((len0, sink0), (len1 - first, sink1))):
            pos = tok + base
            mine = (tok < first) if r == 0 else (tok >= first)
            ok = mine & (slot <= pos) & ((slot < sinks) | (slot > pos - WIN))
            bias_ref[:, r * cap:(r + 1) * cap] = jnp.where(ok, 0.0, -1e30)
        tok = lax.broadcasted_iota(jnp.int32, (cap, rows), 1)
        slot = lax.broadcasted_iota(jnp.int32, (cap, rows), 0)
        for r, base in enumerate((len0, len1 - first)):
            mine = (tok < first) if r == 0 else (tok >= first)
            hot = mine & (slot == tok + base)
            hot_ref[r * cap:(r + 1) * cap, :] = jnp.where(hot, 1.0, 0.0).astype(jnp.bfloat16)

    x = x_ref[...].reshape(rows, width)
    tok = lax.broadcasted_iota(jnp.int32, (rows, HD), 0)
    early = tok < first
    cos = jnp.where(early, cos_ref[pl.ds(len0 + rows, rows), :], cos_ref[pl.ds(len1 - first + rows, rows), :])
    sin = jnp.where(early, sin_ref[pl.ds(len0 + rows, rows), :], sin_ref[pl.ds(len1 - first + rows, rows), :])

    def rotated(v):
        cols = []
        for h in range(HEADS_STEP):
            part = v[:, h * HD:(h + 1) * HD]
            cols.append((part * cos + pltpu.roll(part, HD // 2, 1) * sin).astype(jnp.bfloat16))
        return cols

    q = rotated(jnp.dot(x, w_ref[0], preferred_element_type=jnp.float32))
    k = jnp.concatenate(rotated(jnp.dot(x, w_ref[1], preferred_element_type=jnp.float32)), axis=1)
    v = jnp.dot(x, w_ref[2], preferred_element_type=jnp.float32).astype(jnp.bfloat16)

    for r, (start, count) in enumerate(((len0, first), (len1, second))):
        span = slice(r * cap, (r + 1) * cap)
        slot = lax.broadcasted_iota(jnp.int32, (cap, HEADS_STEP * HD), 0)
        written = (slot >= start) & (slot < start + count)
        hot = hot_ref[span, :]
        new_k = jnp.dot(hot, k, preferred_element_type=jnp.float32)
        nk_ref[span, :] = jnp.where(written, new_k, ck_ref[span, :].astype(jnp.float32)).astype(jnp.bfloat16)
        new_v = jnp.dot(hot, v, preferred_element_type=jnp.float32)
        nv_ref[span, :] = jnp.where(written, new_v, cv_ref[span, :].astype(jnp.float32)).astype(jnp.bfloat16)

    mixed = []
    for h in range(HEADS_STEP):
        cols = slice(h * HD, (h + 1) * HD)
        scores = lax.dot_general(q[h], nk_ref[:, cols], (((1,), (1,)), ((), ())), preferred_element_type=jnp.float32)
        scores = scores * (HD ** (-0.5) * LOG2E) + bias_ref[...]
        top = jnp.max(scores, axis=1, keepdims=True)
        weights = jnp.exp2(scores - top)
        total = jnp.sum(weights, axis=1, keepdims=True)
        part = jnp.dot(weights.astype(jnp.bfloat16), nv_ref[:, cols], preferred_element_type=jnp.float32)
        mixed.append((part / total).astype(jnp.bfloat16))
    acc_ref[...] += jnp.dot(jnp.concatenate(mixed, axis=1), wo_ref[...], preferred_element_type=jnp.float32)

    @pl.when(step == pl.num_programs(0) - 1)
    def _():
        out_ref[...] = acc_ref[...].astype(jnp.bfloat16)


def attention(gathered, marks, rows_dev, lens, sinks, cache_k, cache_v, w_qkv, w_out):
    parts, _, width = gathered.shape
    rows = parts * rows_dev
    reqs, cap, cols = cache_k.shape
    slots = reqs * cap
    step_cols = HEADS_STEP * HD
    cos, sin = rope_table(rows, rows, cap + rows)
    smem = pl.BlockSpec(memory_space=pltpu.SMEM)
    full2 = lambda s: (0, 0)
    nk, nv, out = pl.pallas_call(
        functools.partial(attn_kernel, rows_dev, cap),
        grid=(cols // step_cols,),
        in_specs=[
            smem,
            smem,
            pl.BlockSpec(gathered.shape, lambda s: (0, 0, 0)),
            pl.BlockSpec(marks.shape, lambda s: (0, 0, 0)),
            pl.BlockSpec(cos.shape, full2),
            pl.BlockSpec(sin.shape, full2),
            pl.BlockSpec((3, width, step_cols), lambda s: (0, 0, s)),
            pl.BlockSpec((slots, step_cols), lambda s: (0, s)),
            pl.BlockSpec((slots, step_cols), lambda s: (0, s)),
            pl.BlockSpec((step_cols, width), lambda s: (s, 0)),
        ],
        out_specs=[
            pl.BlockSpec((slots, step_cols), lambda s: (0, s)),
            pl.BlockSpec((slots, step_cols), lambda s: (0, s)),
            pl.BlockSpec((rows, width), full2),
        ],
        out_shape=[
            jax.ShapeDtypeStruct((slots, cols), jnp.bfloat16),
            jax.ShapeDtypeStruct((slots, cols), jnp.bfloat16),
            jax.ShapeDtypeStruct((rows, width), jnp.bfloat16),
        ],
        scratch_shapes=[
            pltpu.VMEM((rows, slots), jnp.float32),
            pltpu.VMEM((slots, rows), jnp.bfloat16),
            pltpu.VMEM((rows, width), jnp.float32),
        ],
        compiler_params=pltpu.CompilerParams(vmem_limit_bytes=56 * 2**20),
        name="attention",
    )(
        lens,
        sinks,
        gathered,
        marks,
        cos,
        sin,
        jnp.transpose(w_qkv, (1, 0, 2)),
        cache_k.reshape(slots, cols),
        cache_v.reshape(slots, cols),
        w_out,
    )
    return nk.reshape(cache_k.shape), nv.reshape(cache_v.shape), out


def expert_kernel(x_ref, gate_ref, w_ref, out_ref):
    x = x_ref[...]
    total = None
    for e in range(w_ref.shape[0]):
        g = jnp.dot(x, w_ref[e, 0], preferred_element_type=jnp.float32)
        u = jnp.dot(x, w_ref[e, 1], preferred_element_type=jnp.float32)
        act = (g / (1.0 + jnp.exp(-g)) * u * gate_ref[:, e:e + 1]).astype(jnp.bfloat16)
        part = lax.dot_general(act, w_ref[e, 2], (((1,), (1,)), ((), ())), preferred_element_type=jnp.float32)
        total = part if total is None else total + part
    out_ref[...] = total.astype(jnp.bfloat16)


def experts(rows, gates, w_expert):
    count, width = rows.shape
    block = 256
    n_exp = w_expert.shape[0]
    return pl.pallas_call(
        expert_kernel,
        grid=(count // block,),
        in_specs=[
            pl.BlockSpec((block, width), lambda i: (i, 0)),
            pl.BlockSpec((block, n_exp), lambda i: (i, 0)),
            pl.BlockSpec(w_expert.shape, lambda i: (0, 0, 0, 0)),
        ],
        out_specs=pl.BlockSpec((block, width), lambda i: (i, 0)),
        out_shape=jax.ShapeDtypeStruct((count, width), jnp.bfloat16),
        compiler_params=pltpu.CompilerParams(vmem_limit_bytes=56 * 2**20),
        name="experts",
    )(rows, gates, w_expert)


MESH = pl.DeviceIdType.MESH
VMEM_LIMIT = 60 * 2**20


def partners():
    head, tok = lax.axis_index("head"), lax.axis_index("tok")
    z, core = tok // 2, tok % 2
    across = [head + 1 - 2 * (head % 2), (head + 2) % 4, 3 - head]
    layer = [{"head": h, "tok": tok} for h in across]
    sibling = {"head": head, "tok": 2 * z + 1 - core}
    column = [{"head": head, "tok": ((z + d) % 4) * 2 + core} for d in range(4)]
    return head, across, layer, sibling, column


def greet(devices):
    barrier = pltpu.get_barrier_semaphore()
    for device in devices:
        pl.semaphore_signal(barrier, inc=1, device_id=device, device_id_type=MESH)
    pl.semaphore_wait(barrier, len(devices))


def head_gather_kernel(tokens_ref, gain_ref, marks_ref, out_ref, all_marks_ref, send_sem, recv_sem):
    head, across, layer, _, _ = partners()
    half = tokens_ref.shape[0] // 2

    def copy(index, src, dst, device):
        return pltpu.make_async_remote_copy(
            src_ref=src, dst_ref=dst, send_sem=send_sem.at[index], recv_sem=recv_sem.at[index],
            device_id=device, device_id_type=MESH)

    out_ref[head] = rms_norm(tokens_ref[...], gain_ref[...]).astype(jnp.bfloat16)
    all_marks_ref[head] = marks_ref[...]
    greet(layer)
    own = out_ref.at[head]
    mark = all_marks_ref.at[head]
    sends = [copy(i, own, own, layer[i]) for i in range(2)] + [copy(4 + i, mark, mark, layer[i]) for i in range(3)]
    for c in sends:
        c.start()
    spans = [pl.ds(0, half), pl.ds(half, half)]
    for i in range(2):
        arrived = out_ref.at[across[i]]
        copy(i, arrived, arrived, layer[i]).wait_recv()
        block = out_ref.at[across[i], spans[i]]
        c = copy(2 + i, block, block, layer[1 - i])
        c.start()
        sends.append(c)
    for i in range(2):
        block = out_ref.at[across[2], spans[i]]
        copy(2 + i, block, block, layer[1 - i]).wait_recv()
    for i in range(3):
        arrived = all_marks_ref.at[across[i]]
        copy(4 + i, arrived, arrived, layer[i]).wait_recv()
    for c in sends:
        c.wait_send()


def head_gather(tokens, gain, marks, parts):
    vmem = pl.BlockSpec(memory_space=pltpu.VMEM)
    return pl.pallas_call(
        head_gather_kernel,
        in_specs=[vmem] * 3,
        out_specs=[vmem] * 2,
        out_shape=[
            jax.ShapeDtypeStruct((parts, *tokens.shape), jnp.bfloat16),
            jax.ShapeDtypeStruct((parts, *marks.shape), jnp.bfloat16),
        ],
        scratch_shapes=[pltpu.SemaphoreType.DMA((7,)), pltpu.SemaphoreType.DMA((7,))],
        compiler_params=pltpu.CompilerParams(collective_id=0, has_side_effects=True, vmem_limit_bytes=VMEM_LIMIT),
        name="head_gather",
    )(tokens, gain.reshape(1, -1), marks)


def layer_kernel(mixed_ref, tokens_ref, gain_ref, gates_ref, w_hbm, out_ref,
                 head_buf, resid, w_ref, x_buf, part, core_buf, diag_buf, side_buf, z_buf, send_sem, recv_sem, w_sem):
    head, across, layer, sibling, column = partners()
    tok = lax.axis_index("tok")
    rows, width = tokens_ref.shape
    n_exp = w_ref.shape[0]
    half = rows // 2
    started = []
    z = tok // 2
    bottom, top = (3 - z) // 3, z // 3
    slots = [0, 1 + 2 * bottom, 3 - bottom - top, 2 - bottom + top]

    def copy(index, src, dst, device, sender=None):
        return pltpu.make_async_remote_copy(
            src_ref=src, dst_ref=dst, send_sem=send_sem.at[index if sender is None else sender],
            recv_sem=recv_sem.at[index], device_id=device, device_id_type=MESH)

    def start(*args):
        c = copy(*args)
        c.start()
        started.append(c)

    def arrived(index, dst, device):
        copy(index, dst, dst, device).wait_recv()

    weights = pltpu.make_async_copy(w_hbm, w_ref, w_sem)
    weights.start()
    greet(layer + [sibling] + column[1:])

    for r in (2, 0, 1):
        start(r, mixed_ref.at[across[r]], head_buf.at[r], layer[r])
    total = tokens_ref[...].astype(jnp.float32)
    mine = mixed_ref[head].astype(jnp.float32)
    for r in range(3):
        arrived(r, head_buf.at[r], layer[r])
        mine = mine + head_buf[r].astype(jnp.float32)
    residual = (total + mine).astype(jnp.bfloat16)
    resid[...] = residual
    x_buf[0, 0, 0, :, :width] = rms_norm(residual, gain_ref[...]).astype(jnp.bfloat16)
    x_buf[0, 0, 0, :, width:] = gates_ref[...]

    low, high = pl.ds(0, half), pl.ds(half, half)

    def along(k, up):
        s = slots[k]
        to = s + 1 if up else (s + 3) % 4
        return copy(2 + to, x_buf.at[0, s, 0], x_buf.at[0, to, 0], column[1 if up else 3], (49 if up else 53) + to)

    def moves(k, up):
        if up:
            return z < 3 if k == 0 else (slots[k] <= z) & (z < 3)
        return z > 0 if k == 0 else (slots[k] > z) & (z > 0)

    def stage_a(k):
        s = slots[k]
        if k:
            arrived(2 + s, x_buf.at[0, s, 0], column[1])
        for up in (True, False):
            pl.when(moves(k, up))(along(k, up).start)
        block = x_buf.at[0, s, 0]
        start(6 + k, block, x_buf.at[0, s, 1], layer[0])
        start(10 + k, block, x_buf.at[0, s, 2], layer[1])

    def stage_b(k):
        s = slots[k]
        arrived(6 + k, x_buf.at[0, s, 1], layer[0])
        start(14 + k, x_buf.at[0, s, 1, low], x_buf.at[0, s, 3, low], layer[1])
        arrived(10 + k, x_buf.at[0, s, 2], layer[1])
        start(18 + k, x_buf.at[0, s, 2, high], x_buf.at[0, s, 3, high], layer[0])

    def stage_c(k):
        s = slots[k]
        arrived(14 + k, x_buf.at[0, s, 3, low], layer[1])
        arrived(18 + k, x_buf.at[0, s, 3, high], layer[0])
        start(22 + k, x_buf.at[0, s], x_buf.at[1, s], sibling)

    def compute(index, k):
        s = slots[k]
        x = x_buf[index, s, :, :, :width].reshape(4 * rows, width)
        gates = x_buf[index, s, :, :, width:].reshape(4 * rows, HD).astype(jnp.float32)
        lane = lax.broadcasted_iota(jnp.int32, gates.shape, 1) % (HD // 2)
        total = None
        for e in range(n_exp):
            gate = jnp.sum(jnp.where(lane == tok * n_exp + e, gates, 0.0), axis=1, keepdims=True)
            g = jnp.dot(x, w_ref[e, 0], preferred_element_type=jnp.float32)
            u = jnp.dot(x, w_ref[e, 1], preferred_element_type=jnp.float32)
            act = (g / (1.0 + jnp.exp(-g)) * u * gate).astype(jnp.bfloat16)
            p = lax.dot_general(act, w_ref[e, 2], (((1,), (1,)), ((), ())), preferred_element_type=jnp.float32)
            total = p if total is None else total + p
        part[index, k] = total.astype(jnp.bfloat16).reshape(4, rows, width)

    def stage_d(s):
        if s == 0:
            weights.wait()
        compute(0, s)
        arrived(22 + s, x_buf.at[1, slots[s]], sibling)
        compute(1, s)
        start(26 + s, part.at[1, s], core_buf.at[s], sibling)

    def add(r, s, other, span=slice(None)):
        part[0, s, r, span, :] = (part[0, s, r, span, :].astype(jnp.float32) + other.astype(jnp.float32)).astype(jnp.bfloat16)

    def stage_e(s):
        arrived(26 + s, core_buf.at[s], sibling)
        add(3, s, core_buf[s, 3])
        start(30 + s, part.at[0, s, 3, low], diag_buf.at[0, s], layer[0])
        start(34 + s, part.at[0, s, 3, high], diag_buf.at[1, s], layer[1])
        for r in range(3):
            add(r, s, core_buf[s, r])

    def stage_f(s):
        arrived(30 + s, diag_buf.at[0, s], layer[0])
        add(2, s, diag_buf[0, s], slice(0, half))
        start(42 + s, part.at[0, s, 2], side_buf.at[1, s], layer[1])
        arrived(34 + s, diag_buf.at[1, s], layer[1])
        add(1, s, diag_buf[1, s], slice(half, rows))
        start(38 + s, part.at[0, s, 1], side_buf.at[0, s], layer[0])

    def stage_g(s):
        arrived(38 + s, side_buf.at[0, s], layer[0])
        arrived(42 + s, side_buf.at[1, s], layer[1])
        add(0, s, side_buf[0, s].astype(jnp.float32) + side_buf[1, s].astype(jnp.float32))
        if s:
            slot = slots[s]
            owner = {"head": head, "tok": ((z + 4 - slot) % 4) * 2 + tok % 2}
            start(45 + slot, part.at[0, s, 0], z_buf.at[slot], owner)

    a, b, c, d, e, f, g = stage_a, stage_b, stage_c, stage_d, stage_e, stage_f, stage_g
    plan = ((a, 0), (a, 1), (b, 0), (a, 2), (c, 0), (d, 0), (a, 3), (b, 1), (c, 1), (b, 2), (d, 1), (c, 2), (b, 3), (e, 1), (d, 2), (f, 1), (c, 3), (e, 2), (d, 3), (f, 2), (e, 3), (g, 1), (f, 3), (e, 0), (g, 2), (f, 0), (g, 3), (g, 0),)
    for stage, s in plan:
        stage(s)

    total = part[0, 0, 0].astype(jnp.float32)
    for s in (1, 3, 2):
        arrived(45 + s, z_buf.at[s], column[s])
        total = total + z_buf[s].astype(jnp.float32)
    out_ref[...] = (resid[...].astype(jnp.float32) + total).astype(jnp.bfloat16)
    for c in started:
        c.wait_send()
    for k in range(4):
        for up in (True, False):
            pl.when(moves(k, up))(along(k, up).wait_send)


def layer_rest(mixed, tokens, gain, gates, w_expert):
    rows, width = tokens.shape
    vmem = pl.BlockSpec(memory_space=pltpu.VMEM)
    bf16 = jnp.bfloat16
    return pl.pallas_call(
        layer_kernel,
        in_specs=[vmem] * 4 + [pl.BlockSpec(memory_space=pl.ANY)],
        out_specs=vmem,
        out_shape=jax.ShapeDtypeStruct((rows, width), bf16),
        scratch_shapes=[
            pltpu.VMEM((3, rows, width), bf16),
            pltpu.VMEM((rows, width), bf16),
            pltpu.VMEM(w_expert.shape, bf16),
            pltpu.VMEM((2, 4, 4, rows, width + HD), bf16),
            pltpu.VMEM((2, 4, 4, rows, width), bf16),
            pltpu.VMEM((4, 4, rows, width), bf16),
            pltpu.VMEM((2, 4, rows // 2, width), bf16),
            pltpu.VMEM((2, 4, rows, width), bf16),
            pltpu.VMEM((4, rows, width), bf16),
            pltpu.SemaphoreType.DMA((57,)),
            pltpu.SemaphoreType.DMA((49,)),
            pltpu.SemaphoreType.DMA,
        ],
        compiler_params=pltpu.CompilerParams(collective_id=1, has_side_effects=True, vmem_limit_bytes=VMEM_LIMIT),
        name="layer_rest",
    )(mixed.reshape(-1, rows, width), tokens, gain.reshape(1, -1), gates, w_expert)


def on_device(
    tokens,
    token_req,
    cache_len,
    sink_count,
    cache_k,
    cache_v,
    attn_gain,
    w_qkv,
    w_out,
    ffn_gain,
    routes,
    route_weight,
    w_expert,
):
    tok_dev, width = tokens.shape
    exp_dev = w_expert.shape[0]
    expert_total = exp_dev * lax.axis_size("tok")
    direct = lax.axis_size("tok") == 8 and lax.axis_size("head") == 4
    marks = jnp.zeros((PAD, HD), jnp.bfloat16).at[0, :tok_dev].set(token_req.astype(jnp.bfloat16))
    chosen = routes[:, :, None] == jnp.arange(expert_total, dtype=jnp.int32)[None, None, :]
    gates = jnp.sum(jnp.where(chosen, route_weight[:, :, None], 0.0), axis=1)
    if direct:
        gathered, marks = head_gather(tokens, attn_gain, marks, lax.axis_size("head"))
    else:
        normed = rms_norm(tokens, attn_gain).astype(jnp.bfloat16)
        gathered = lax.all_gather(normed, "head", axis=0)
        marks = lax.all_gather(marks, "head", axis=0)
    new_k, new_v, mixed = attention(gathered, marks, tok_dev, cache_len, sink_count, cache_k, cache_v, w_qkv, w_out)
    if direct:
        gates = jnp.pad(gates, ((0, 0), (0, HD // 2 - expert_total)))
        rounded = lax.reduce_precision(gates, 8, 7)
        sent = jnp.concatenate([rounded, gates - rounded], axis=1).astype(jnp.bfloat16)
        return (layer_rest(mixed, tokens, ffn_gain, sent, w_expert), new_k, new_v)
    gates = lax.all_gather(gates, ("tok", "head"), axis=0, tiled=True)
    gates = lax.dynamic_slice_in_dim(gates, lax.axis_index("tok") * exp_dev, exp_dev, axis=1)
    mixed = lax.psum_scatter(mixed, "head", scatter_dimension=0, tiled=True)
    residual = (tokens.astype(jnp.float32) + mixed.astype(jnp.float32)).astype(jnp.bfloat16)
    ffn_input = rms_norm(residual, ffn_gain).astype(jnp.bfloat16)
    rows = lax.all_gather(ffn_input, ("tok", "head"), axis=0, tiled=True)
    partial = experts(rows, gates, w_expert)
    combined = lax.psum_scatter(partial, ("tok", "head"), scatter_dimension=0, tiled=True)
    hidden_out = (residual.astype(jnp.float32) + combined.astype(jnp.float32)).astype(jnp.bfloat16)
    return (hidden_out, new_k, new_v)


def solution(mesh):
    return jax.shard_map(
        on_device,
        mesh=mesh,
        in_specs=(
            P(("tok", "head"), None),
            P(("tok", "head")),
            P("tok"),
            P("tok"),
            P("tok", None, "head"),
            P("tok", None, "head"),
            P(),
            P(None, None, "head"),
            P("head", None),
            P(),
            P(("tok", "head"), None),
            P(("tok", "head"), None),
            P("tok", None, None, "head"),
        ),
        out_specs=(P(("tok", "head"), None), P("tok", None, "head"), P("tok", None, "head")),
        check_vma=False,
    )
```
